256 devices in a mesh: seq: 16 (over x_lo, z), dp: 16 (over x_hi, y, core).
Axes of the slice: x: 4 (x_hi: 2, x_lo: 2; x = x_hi * 2 + x_lo), y: 4, z: 8, core: 2. Of those that a mesh axis runs over, the one named last changes fastest.
Arguments:
- self_query: bfloat16 [16, 2048, 2048], P('dp', 'seq'), may hold values from -13 to 13
- self_key: bfloat16 [16, 2048, 2048], P('dp', 'seq'), may hold values from -10 to 10
- self_value: bfloat16 [16, 2048, 2048], P('dp', 'seq'), may hold values from -6 to 6
- cross_query: bfloat16 [16, 2048, 2048], P('dp', 'seq'), may hold values from -6 to 6
- upstream: bfloat16 [16, 2048, 2048], P('dp', 'seq'), may hold values from -6 to 6
- caption_ids: int32 [16, 512], replicated, may hold values from 0 to 16383
- caption_lengths: int32 [16], replicated, may hold values from 64 to 512, as said below
- embed_table: bfloat16 [16384, 4096], P('dp', 'seq'), may hold values from -134 to 134
- key_weight: bfloat16 [4096, 2048], P(None, 'seq'), may hold values from -0.09375 to 0.09375
- value_weight: bfloat16 [4096, 2048], P(None, 'seq'), may hold values from -0.09375 to 0.09375
Outputs:
- grad_query: bfloat16 [16, 2048, 2048], P('dp', 'seq')
- grad_key: bfloat16 [16, 2048, 2048], P('dp', 'seq')
- grad_value: bfloat16 [16, 2048, 2048], P('dp', 'seq')
- grad_cross_query: bfloat16 [16, 2048, 2048], P('dp', 'seq')
- grad_key_weight: bfloat16 [4096, 2048], P(None, 'seq')
- grad_value_weight: bfloat16 [4096, 2048], P(None, 'seq')
The draws below stay inside these ranges and needn't reach their ends.
Inputs may be any that keep to these rules, and one draw needn't show every extreme that they name: `caption_lengths`: some clip has exactly 512 live caption tokens and some other clip exactly 64.
All inputs are finite; a program needn't handle non-finite values.
Results may differ from the reference program's by a relative error of at most 0.024.
Values may be sent and summed in bfloat16 or wider, within the bound.
A program may use at most 128 MiB of HBM per device.

```python
import math
import jax
import jax.numpy as jnp
import numpy as np
from jax import lax

HEADS = 16
HEAD_DIM = 128
DT = 4096
VOCAB = 16384
CAP = 512
SEQ_LEN = 2048
CLIPS = 16


def draw_self_query(key, part):
    key = jax.random.fold_in(key, 1)
    own = jax.random.normal(key, (CLIPS, SEQ_LEN, HEADS * HEAD_DIM), jnp.float32)
    return jnp.clip(own, -4.0, 4.0).astype(jnp.bfloat16)


def draw_self_key(key, part):
    key = jax.random.fold_in(key, 2)
    own = jax.random.normal(key, (CLIPS, SEQ_LEN, HEADS * HEAD_DIM), jnp.float32)
    return jnp.clip(own, -4.0, 4.0).astype(jnp.bfloat16)


def draw_caption_lengths(key, part):
    key = jax.random.fold_in(key, 3)
    first, second, third = jax.random.split(key, 3)
    lengths = jax.random.randint(first, (CLIPS,), CAP // 8, CAP + 1, jnp.int32)
    longest = jax.random.randint(second, (), 0, CLIPS, jnp.int32)
    shortest = (longest + 1 + jax.random.randint(third, (), 0, CLIPS - 1, jnp.int32)) % CLIPS
    return lengths.at[shortest].set(CAP // 8).at[longest].set(CAP)


def draw_embed_table(key, part):
    key = jax.random.fold_in(key, 4)
    first, second, third = jax.random.split(key, 3)
    row_scale = jnp.exp(jax.random.uniform(first, (VOCAB, 1), jnp.float32, 0.0, math.log(10.0)))
    column_scale = jnp.exp(jax.random.uniform(second, (1, DT), jnp.float32, 0.0, math.log(10.0)))
    values = jnp.clip(jax.random.normal(third, (VOCAB, DT), jnp.float32), -4.0, 4.0)
    return (values * row_scale * column_scale / 3.0).astype(jnp.bfloat16)


def set_ends(values, key, low, largest):
    extent = values.shape
    place = [jax.random.randint(jax.random.fold_in(key, axis), (), 0, extent[axis]) for axis in range(len(extent))]
    values = values.at[tuple(place)].set(low)
    longest = extent.index(max(extent))
    place[longest] = (place[longest] + 1) % extent[longest]
    return values.at[tuple(place)].set(largest)


def block_scale(own_key, shape, cuts, least, top_value):
    level, own = 1.0, jax.random.fold_in(own_key, 6)
    for axis_at, blocks in cuts:
        draws = jnp.exp(jax.random.uniform(jax.random.fold_in(own, axis_at), (blocks,), jnp.float32, least / len(cuts), top_value / len(cuts)))
        level = level * jnp.repeat(draws, shape[axis_at] // blocks).reshape([-1 if axis == axis_at else 1 for axis in range(len(shape))])
    return level


def cumulative_ranks(amount, lean):
    loads = [(1 << 20) // math.isqrt(grade ** lean) + 1 for grade in range(1, amount + 1)]
    spread = 1 + sum(loads) // (1 << 30)
    return np.cumsum(np.array([max(1, weight // spread) for weight in loads]))


def ranked_ids(own_key, dims, amount, slope):
    grid = cumulative_ranks(amount, slope)
    ticket = jax.random.randint(jax.random.fold_in(own_key, 1), dims, 0, int(grid[amount - 1]))
    grade = jnp.searchsorted(jnp.asarray(grid, jnp.int32), ticket, side="right")
    return jax.random.permutation(jax.random.fold_in(own_key, 2), amount)[grade].astype(jnp.int32)


def normal_values(stream_key, shape, deviation, reach, pieces=(), kind=jnp.bfloat16):
    result = jax.random.normal(stream_key, shape, jnp.float32) * deviation
    if len(pieces) > 0:
        result = block_scale(stream_key, shape, pieces, -0.22, 0.18) * result
    return jnp.clip(result, min=-reach, max=reach).astype(kind)


def setup_inputs(seed: int = 0) -> dict:
    splits = jax.random.split(jax.random.key(seed), 11)
    return {
        "self_query": draw_self_query(jax.random.fold_in(splits[10], 71), 0),
        "self_key": draw_self_key(jax.random.fold_in(splits[10], 71), 0),
        "self_value": normal_values(splits[2], (CLIPS, SEQ_LEN, HEADS * HEAD_DIM), 1.0, 6.0, ((0, 16), (1, 16))),
        "cross_query": normal_values(splits[3], (CLIPS, SEQ_LEN, HEADS * HEAD_DIM), 1.0, 6.0, ((0, 16), (1, 16))),
        "upstream": normal_values(splits[4], (CLIPS, SEQ_LEN, HEADS * HEAD_DIM), 1.0, 6.0, ((0, 16), (1, 16))),
        "caption_ids": set_ends(ranked_ids(splits[5], (CLIPS, CAP), VOCAB, 1), jax.random.fold_in(splits[5], 3), 0, VOCAB - 1).astype(jnp.int32),
        "caption_lengths": draw_caption_lengths(jax.random.fold_in(splits[10], 71), 0),
        "embed_table": draw_embed_table(jax.random.fold_in(splits[10], 71), 0),
        "key_weight": normal_values(splits[8], (DT, HEADS * HEAD_DIM), DT ** -0.5, 0.09375, ((1, 16),)),
        "value_weight": normal_values(splits[9], (DT, HEADS * HEAD_DIM), DT ** -0.5, 0.09375, ((1, 16),)),
    }


def attend_grads(query, keys, values, upstream, key_count):
    row_count = query.shape[0]
    head_width = query.shape[1]
    block_rows = math.gcd(row_count, 512)
    scaling = head_width ** (-0.5)
    live_keys = jnp.arange(keys.shape[0], dtype=jnp.int32) < key_count

    def step(totals, block_index):
        row_start = block_index * block_rows
        query_part = lax.dynamic_slice_in_dim(query, row_start, block_rows, 0)
        upstream_part = lax.dynamic_slice_in_dim(upstream, row_start, block_rows, 0)
        scores = jnp.dot(query_part, keys.T, preferred_element_type=jnp.float32) * scaling
        scores = jnp.where(live_keys[None, :], scores, -jnp.inf)
        row_top = lax.optimization_barrier(jnp.max(scores, axis=1, keepdims=True))
        exponent = jnp.exp(scores - row_top)
        probs_full = exponent / lax.optimization_barrier(jnp.sum(exponent, axis=1, keepdims=True))
        probs_low = probs_full.astype(jnp.bfloat16)
        attended = jnp.dot(probs_low, values, preferred_element_type=jnp.float32)
        row_delta = lax.optimization_barrier(jnp.sum(upstream_part.astype(jnp.float32) * attended, axis=1, keepdims=True))
        dprobs = jnp.dot(upstream_part, values.T, preferred_element_type=jnp.float32)
        dscores = (probs_full * (dprobs - row_delta)).astype(jnp.bfloat16)
        query_grad = jnp.dot(dscores, keys, preferred_element_type=jnp.float32) * scaling
        key_total = totals[0] + jnp.dot(dscores.T, query_part, preferred_element_type=jnp.float32) * scaling
        value_total = totals[1] + jnp.dot(probs_low.T, upstream_part, preferred_element_type=jnp.float32)
        return ((key_total, value_total), query_grad)
    zeros_init = jnp.zeros(keys.shape, jnp.float32)
    totals, query_grads = lax.scan(step, (zeros_init, zeros_init), jnp.arange(row_count // block_rows, dtype=jnp.int32))
    return (query_grads.reshape(row_count, head_width), totals[0], totals[1])

def split_heads(matrix):
    return matrix.reshape(matrix.shape[0], HEADS, HEAD_DIM).transpose(1, 0, 2)

def join_heads(stacked):
    return stacked.transpose(1, 0, 2).reshape(stacked.shape[1], HEADS * HEAD_DIM)

def reference(self_query, self_key, self_value, cross_query, upstream, caption_ids, caption_lengths, embed_table, key_weight, value_weight):

    def pick(array, clip_index):
        return lax.dynamic_index_in_dim(array, clip_index, 0, keepdims=False)

    def per_clip(totals, clip_index):
        id_row = pick(caption_ids, clip_index)
        embedded = jnp.take(embed_table, id_row, axis=0)
        mean_square = lax.optimization_barrier(jnp.mean(embedded.astype(jnp.float32) ** 2, axis=1, keepdims=True))
        rinv = lax.rsqrt(mean_square + 1e-06)
        cross_key = (jnp.dot(embedded, key_weight, preferred_element_type=jnp.float32) * rinv).astype(jnp.bfloat16)
        cross_value = (jnp.dot(embedded, value_weight, preferred_element_type=jnp.float32) * rinv).astype(jnp.bfloat16)
        upstream_heads = split_heads(pick(upstream, clip_index))
        self_grads = jax.vmap(attend_grads, in_axes=(0, 0, 0, 0, None))(split_heads(pick(self_query, clip_index)), split_heads(pick(self_key, clip_index)), split_heads(pick(self_value, clip_index)), upstream_heads, jnp.int32(SEQ_LEN))
        live_count = pick(caption_lengths, clip_index)
        cross_grads = jax.vmap(attend_grads, in_axes=(0, 0, 0, 0, None))(split_heads(pick(cross_query, clip_index)), split_heads(cross_key), split_heads(cross_value), upstream_heads, live_count)
        key_term = (join_heads(cross_grads[1]) * rinv).astype(jnp.bfloat16)
        value_term = (join_heads(cross_grads[2]) * rinv).astype(jnp.bfloat16)
        key_total = totals[0] + jnp.dot(embedded.T, key_term, preferred_element_type=jnp.float32)
        value_total = totals[1] + jnp.dot(embedded.T, value_term, preferred_element_type=jnp.float32)
        outputs = (join_heads(self_grads[0]).astype(jnp.bfloat16), join_heads(self_grads[1]).astype(jnp.bfloat16), join_heads(self_grads[2]).astype(jnp.bfloat16), join_heads(cross_grads[0]).astype(jnp.bfloat16))
        return ((key_total, value_total), outputs)
    zeros_init = jnp.zeros((DT, HEADS * HEAD_DIM), jnp.float32)
    totals, outputs = lax.scan(per_clip, (zeros_init, zeros_init), jnp.arange(CLIPS, dtype=jnp.int32))
    return (outputs[0], outputs[1], outputs[2], outputs[3], totals[0].astype(jnp.bfloat16), totals[1].astype(jnp.bfloat16))
```

```python
import math

import jax
import jax.numpy as jnp
from jax import lax
from jax.experimental import pallas as pl
from jax.experimental.pallas import tpu as pltpu
from jax.sharding import PartitionSpec as P

MESH = pl.DeviceIdType.MESH
BF = jnp.bfloat16
F32 = jnp.float32

NZ = 8
NS = 2 * NZ
NY = 4
HD = 128
TB = 128
T = NS * TB
CAP = 512
CW = 256
HC = CW // 2
VR = 1024
BQ = 256
NQ = T // BQ
KC = 256
SCALE = HD**-0.5
LOG2 = SCALE * math.log2(math.e)


def nt(a, b):
    return lax.dot_general(a, b, (((1,), (1,)), ((), ())), preferred_element_type=F32)


def mm(a, b):
    return jnp.dot(a, b, preferred_element_type=F32)


def fold(x, op):
    return op(x.reshape(x.shape[0] // 8, 8, x.shape[1]), axis=0)


def kernel(
    sq, sk, sv, cq, up, ids, lens, table, kw, vw,
    oq, ok, ov, oc, gk, gv,
    abuf, tabt, part, relay, rsy, rsx, emb, wt, wbuf, s_ref, e_ref, l_ref, kt, acc,
    dbuf, ckv, ckt, term, wsib, wcore, wown, wfar, wstep, wrelay, wry, wxs, wrx, agw,
    a_send, a_recv, loc, t_sem, y_send, y_recv, g_send, g_recv, o_send, o_recv, w_send, w_recv,
):
    me = lax.axis_index("seq")
    my_dp = lax.axis_index("dp")
    xl, z = me // NZ, me % NZ
    core = my_dp % 2
    chip = my_dp // 2
    xh, y = chip // NY, chip % NY

    def dp_of(x_at, y_at, c_at):
        return (x_at * NY + y_at) * 2 + c_at

    y_next, y_prev, y_far = (y + 1) % NY, (y + NY - 1) % NY, (y + 2) % NY
    sib = {"dp": dp_of(xh, y, 1 - core)}
    up_y = {"dp": dp_of(xh, y_next, core)}
    down_y = {"dp": dp_of(xh, y_prev, core)}
    over_x = {"dp": dp_of(1 - xh, y, core)}
    up_z = {"seq": xl * NZ + (z + 1) % NZ}
    down_z = {"seq": xl * NZ + (z + NZ - 1) % NZ}
    over_l = {"seq": (1 - xl) * NZ + z}

    def remote(src, dst, send, recv, device):
        return pltpu.make_async_remote_copy(
            src_ref=src, dst_ref=dst, send_sem=send, recv_sem=recv, device_id=device, device_id_type=MESH
        )

    barrier = pltpu.get_barrier_semaphore()

    def greet(k, carry):
        pl.semaphore_signal(barrier, inc=1, device_id={"seq": (me + k) % NS}, device_id_type=MESH)
        return carry

    lax.fori_loop(1, NS, greet, 0)
    for other in (sib, up_y, down_y, over_x):
        pl.semaphore_signal(barrier, inc=1, device_id=other, device_id_type=MESH)
    pl.semaphore_wait(barrier, NS - 1 + 4)

    tabt[core] = table[...].T
    tab_copy = remote(tabt.at[core], tabt.at[core], t_sem.at[0], t_sem.at[1], sib)
    tab_copy.start()

    mine = pl.ds(pl.multiple_of(me * TB, TB), TB)
    sources = (sq, sk, up, sv, cq)
    for a, src in enumerate(sources):

        def send(k, carry, a=a, src=src):
            peer = (me + k) % NS
            remote(
                src.at[:, pl.ds(pl.multiple_of(peer * HD, HD), HD)],
                abuf.at[a, mine],
                a_send.at[a],
                a_recv.at[a],
                {"seq": peer},
            ).start()
            return carry

        lax.fori_loop(1, NS, send, 0)
        pltpu.make_async_copy(
            src.at[:, pl.ds(pl.multiple_of(me * HD, HD), HD)], abuf.at[a, mine], loc.at[a]
        ).start()
    w_in = [pltpu.make_async_copy(w, wbuf.at[i], loc.at[5 + i]) for i, w in enumerate((kw, vw))]
    for copy in w_in:
        copy.start()

    def arrived(a):
        most = abuf.at[a, pl.ds(0, T - TB)]
        pltpu.make_async_copy(most, most, a_recv.at[a]).wait()
        pltpu.make_async_copy(
            sources[a].at[:, pl.ds(pl.multiple_of(me * HD, HD), HD)], abuf.at[a, mine], loc.at[a]
        ).wait()

    tab_copy.wait()
    rows = lax.broadcasted_iota(jnp.int32, (KC, CAP), 0)

    def look(y_at):
        def body(x_at, carry):
            clip = dp_of(x_at, y_at, core)
            wanted = ids[pl.ds(clip, 1), :] - chip * (2 * VR)
            total = jnp.zeros((CW, CAP), F32)
            for half in range(2):
                for v in range(VR // KC):
                    hot = jnp.where(rows == wanted - (half * VR + v * KC), 1.0, 0.0).astype(BF)
                    total += mm(tabt[half, :, v * KC : (v + 1) * KC], hot)
            part[y_at, x_at] = total.astype(BF)
            return carry

        lax.fori_loop(0, 2, body, 0)

    low, high = pl.ds(0, HC), pl.ds(HC, HC)
    look(y_far)
    far_up = remote(part.at[y_far, :, high], relay.at[0], y_send.at[0], y_recv.at[0], up_y)
    far_down = remote(part.at[y_far, :, low], relay.at[1], y_send.at[1], y_recv.at[1], down_y)
    far_up.start()
    far_down.start()
    look(y_next)
    look(y_prev)
    far_up.wait_recv()
    part[y_next, :, HC:] = part[y_next, :, HC:] + relay[0]
    near_up = remote(part.at[y_next], rsy.at[0], y_send.at[2], y_recv.at[2], up_y)
    near_up.start()
    far_down.wait_recv()
    part[y_prev, :, :HC] = part[y_prev, :, :HC] + relay[1]
    near_down = remote(part.at[y_prev], rsy.at[1], y_send.at[3], y_recv.at[3], down_y)
    near_down.start()
    look(y)

    for i, copy in enumerate(w_in):
        copy.wait()
        for j in range(NS):
            wt[i * HD : (i + 1) * HD, j * CW : (j + 1) * CW] = wbuf[i, j * CW : (j + 1) * CW, :].T

    near_up.wait_recv()
    near_down.wait_recv()
    part[y, 1 - xh] = part[y, 1 - xh] + rsy[0, 1 - xh] + rsy[1, 1 - xh]
    x_copy = remote(part.at[y, 1 - xh], rsx, y_send.at[4], y_recv.at[4], over_x)
    x_copy.start()
    part[y, xh] = part[y, xh] + rsy[0, xh] + rsy[1, xh]

    def col(x_at, shift):
        return x_at * NZ + (z + shift + NZ) % NZ

    messages = {}

    def go(name, slot, part_rows, device):
        i = len(messages)
        ref = emb.at[slot] if part_rows is None else emb.at[slot, part_rows]
        messages[name] = remote(ref, ref, g_send.at[i], g_recv.at[i], device)
        messages[name].start()

    def got(name):
        messages[name].wait_recv()

    ox = 1 - xl

    def gather_start():
        x_copy.wait_recv()
        emb[me] = part[y, xh] + rsx[...]
        go("xb", me, high, over_l)
        go("p1", me, None, up_z)
        go("m1", me, None, down_z)
        go("xa", me, low, over_l)

    def gather_step(k):
        if k == 0:
            got("xb")
        else:
            got(f"pb{k}")
            got(f"mb{k}")
        if k < 3:
            go(f"pb{k + 1}", col(ox, -k), high, up_z)
            go(f"mb{k + 1}", col(ox, k), high, down_z)
        else:
            go("pb4", col(ox, -3), pl.ds(HC, HC // 2), up_z)
            go("mb4", col(ox, 3), pl.ds(HC + HC // 2, HC // 2), down_z)
        if k > 0:
            got(f"p{k}")
            got(f"m{k}")
            if k < 3:
                go(f"p{k + 1}", col(xl, -k), None, up_z)
                go(f"m{k + 1}", col(xl, k), None, down_z)
            else:
                go("p4", col(xl, -3), low, up_z)
                go("m4", col(xl, 3), high, down_z)
            go(f"fp{k}", col(xl, -k), low, over_l)
            go(f"fm{k}", col(xl, k), low, over_l)

    def gather_last():
        got("p4")
        go("f4", col(xl, 4), low, over_l)

    def gather_end():
        for name in ("xa", "pb4", "mb4", "m4", "fp1", "fm1", "fp2", "fm2", "fp3", "fm3", "f4"):
            got(name)

    def scores(queries, keys, n_keys, live):
        top = jnp.full((8, BQ), -jnp.inf, F32)
        for k in range(n_keys // KC):
            s = nt(keys[k * KC : (k + 1) * KC, :], queries)
            if live is not None:
                at = lax.broadcasted_iota(jnp.int32, (KC, BQ), 0) + k * KC
                s = jnp.where(at < live, s, -jnp.inf)
            s_ref[k * KC : (k + 1) * KC, :] = s
            top = jnp.maximum(top, fold(s, jnp.max))
        top = jnp.max(top, axis=0, keepdims=True) * LOG2
        total = jnp.zeros((8, BQ), F32)
        for k in range(n_keys // KC):
            e = jnp.exp2(s_ref[k * KC : (k + 1) * KC, :] * LOG2 - top)
            total += fold(e, jnp.sum)
            yield e.astype(BF)
        yield jnp.sum(total, axis=0, keepdims=True)

    def grads(queries, upstream, keys_t, values, n_keys, probs, total):
        inv = 1.0 / total
        delta = jnp.zeros((8, BQ), F32)
        for k in range(n_keys // KC):
            dp = nt(values[k * KC : (k + 1) * KC, :], upstream)
            s_ref[k * KC : (k + 1) * KC, :] = dp
            delta += fold(dp * probs[k * KC : (k + 1) * KC, :].astype(F32), jnp.sum)
        delta = jnp.sum(delta, axis=0, keepdims=True) * inv
        inv_rows = jnp.broadcast_to(inv, (HD, BQ)).T
        queries = (queries.astype(F32) * inv_rows).astype(BF)
        upstream = (upstream.astype(F32) * inv_rows).astype(BF)
        dq = jnp.zeros((HD, BQ), F32)
        for k in range(n_keys // KC):
            at = slice(k * KC, (k + 1) * KC)
            e = probs[at, :]
            ds = (e.astype(F32) * (s_ref[at, :] - delta)).astype(BF)
            dq += mm(keys_t[:, at], ds)
            acc[0, at, :] += mm(ds, queries)
            acc[1, at, :] += mm(e, upstream)
        return (dq * (inv * SCALE)).T.astype(BF)

    outs = (oq, ok, ov, oc)

    def post(a, peer):
        src = dbuf.at[a, pl.ds(pl.multiple_of(peer * TB, TB), TB)]
        dst = outs[a].at[:, pl.ds(pl.multiple_of(me * HD, HD), HD)]

        @pl.when(peer != me)
        def _():
            remote(src, dst, o_send.at[a], o_recv.at[a], {"seq": peer}).start()

        @pl.when(peer == me)
        def _():
            pltpu.make_async_copy(src, dst, loc.at[7 + a]).start()

    def first(q, carry):
        at = pl.ds(pl.multiple_of(q * BQ, BQ), BQ)
        for k, e in enumerate(scores(abuf[0, at, :], abuf.at[1], T, None)):
            if k < T // KC:
                e_ref[q, k * KC : (k + 1) * KC, :] = e
            else:
                l_ref[q] = e
        return carry

    def second(q, carry):
        at = pl.ds(pl.multiple_of(q * BQ, BQ), BQ)
        dbuf[0, at, :] = grads(
            abuf[0, at, :], abuf[2, at, :], kt, abuf.at[3], T, e_ref.at[q], l_ref[q]
        )
        for i in range(BQ // TB):
            post(0, q * (BQ // TB) + i)
        return carry

    arrived(0)
    arrived(1)
    for k in range(T // KC):
        kt[:, k * KC : (k + 1) * KC] = abuf[1, k * KC : (k + 1) * KC, :].T
    lax.fori_loop(0, NQ // 2, first, 0)
    gather_start()
    lax.fori_loop(NQ // 2, NQ, first, 0)
    gather_step(0)
    arrived(2)
    arrived(3)
    acc[...] = jnp.zeros_like(acc)
    lax.fori_loop(0, 2, second, 0)
    gather_step(1)
    lax.fori_loop(2, 4, second, 0)
    gather_step(2)
    lax.fori_loop(4, 6, second, 0)
    gather_step(3)
    lax.fori_loop(6, 8, second, 0)
    gather_last()

    dbuf[1] = (acc[0] * SCALE).astype(BF)
    dbuf[2] = acc[1].astype(BF)

    def post_kv(k, carry):
        peer = (me + k) % NS
        post(1, peer)
        post(2, peer)
        return carry

    lax.fori_loop(0, NS, post_kv, 0)

    gather_end()
    square = jnp.zeros((8, CAP), F32)
    kv = jnp.zeros((2 * HD, CAP), F32)
    for j in range(NS):
        block = emb[j]
        kv += mm(wt[:, j * CW : (j + 1) * CW], block)
        wide = block.astype(F32)
        square += fold(wide * wide, jnp.sum)
    mean = jnp.sum(square, axis=0, keepdims=True) * (1.0 / (NS * CW))
    rinv = lax.rsqrt(mean + 1e-06)
    kv = kv * rinv
    ckt[...] = kv[:HD, :].astype(BF)
    ckv[0] = kv[:HD, :].T.astype(BF)
    ckv[1] = kv[HD:, :].T.astype(BF)
    rinv_rows = jnp.broadcast_to(rinv, (HD, CAP)).T

    arrived(4)
    acc[:, :CAP, :] = jnp.zeros((2, CAP, HD), F32)
    live = lens[my_dp]

    def cross(q, carry):
        at = pl.ds(pl.multiple_of(q * BQ, BQ), BQ)
        queries = abuf[4, at, :]
        total = None
        for k, e in enumerate(scores(queries, ckv.at[0], CAP, live)):
            if k < CAP // KC:
                e_ref[0, k * KC : (k + 1) * KC, :] = e
            else:
                total = e
        dbuf[3, at, :] = grads(
            queries, abuf[2, at, :], ckt, ckv.at[1], CAP, e_ref.at[0], total
        )
        for i in range(BQ // TB):
            post(3, q * (BQ // TB) + i)
        return carry

    lax.fori_loop(0, NQ, cross, 0)

    term[:, :HD] = (acc[0, :CAP, :] * SCALE * rinv_rows).astype(BF)
    term[:, HD:] = (acc[1, :CAP, :] * rinv_rows).astype(BF)

    w_messages = []

    def hand(src, dst, device):
        i = len(w_messages)
        w_messages.append(remote(src, dst, w_send.at[i], w_recv.at[i], device))
        w_messages[i].start()
        return w_messages[i]

    def partial(base, out):
        def body(i, carry):
            out[i // 2, i % 2] = mm(emb[base + i], term[...]).astype(out.dtype)
            return carry

        lax.fori_loop(0, NZ, body, 0)

    partial((1 - core) * NZ, wsib)
    to_sib = hand(wsib, wcore, sib)
    partial(core * NZ, wown)
    to_sib.wait_recv()
    wown[...] = wown[...] + wcore[...].astype(F32)
    wfar[...] = wown[y_far].astype(BF)
    f_up = hand(wfar.at[:, high], wrelay.at[0], up_y)
    f_down = hand(wfar.at[:, low], wrelay.at[1], down_y)
    f_up.wait_recv()
    wstep[0, :, :HC] = wown[y_next, :, :HC].astype(BF)
    wstep[0, :, HC:] = (wown[y_next, :, HC:] + wrelay[0].astype(F32)).astype(BF)
    n_up = hand(wstep.at[0], wry.at[0], up_y)
    f_down.wait_recv()
    wstep[1, :, :HC] = (wown[y_prev, :, :HC] + wrelay[1].astype(F32)).astype(BF)
    wstep[1, :, HC:] = wown[y_prev, :, HC:].astype(BF)
    n_down = hand(wstep.at[1], wry.at[1], down_y)
    n_up.wait_recv()
    n_down.wait_recv()

    def here(x_at):
        return wown[y, x_at] + wry[0, x_at].astype(F32) + wry[1, x_at].astype(F32)

    wxs[...] = here(1 - xh).astype(BF)
    x_half = hand(wxs, wrx, over_x)
    mine_sum = here(xh)
    x_half.wait_recv()
    agw[core, y, xh] = (mine_sum + wrx[...].astype(F32)).astype(BF)
    own = agw.at[core, y, xh]
    x_back = hand(own, own, over_x)
    x_back.wait_recv()
    row = agw.at[core, y]
    b_up = hand(row, row, up_y)
    b_down = hand(row, row, down_y)
    backs = [hand(row, row, sib)]
    b_up.wait_recv()
    upper = agw.at[core, y_prev, :, high]
    c_up = hand(upper, upper, up_y)
    b_down.wait_recv()
    lower = agw.at[core, y_next, :, low]
    c_down = hand(lower, lower, down_y)
    for at in (y_prev, y_next):
        backs.append(hand(agw.at[core, at], agw.at[core, at], sib))
    c_up.wait_recv()
    c_down.wait_recv()
    backs.append(hand(agw.at[core, y_far], agw.at[core, y_far], sib))
    for message in backs:
        message.wait_recv()
    leave = [
        pltpu.make_async_copy(agw.at[:, :, :, :, i * HD : (i + 1) * HD], dst, loc.at[11 + i])
        for i, dst in enumerate((gk, gv))
    ]
    for copy in leave:
        copy.start()

    for copy in leave:
        copy.wait()
    tabless = (far_up, far_down, near_up, near_down, x_copy)
    for message in (*tabless, *messages.values(), *w_messages):
        message.wait_send()
    most = abuf.at[0, pl.ds(0, T - TB)]
    for a in range(5):
        pltpu.make_async_copy(most, most, a_send.at[a]).wait()
    for a in range(4):
        pltpu.make_async_copy(most, most, o_send.at[a]).wait()
        pltpu.make_async_copy(most, most, o_recv.at[a]).wait()
        src = dbuf.at[a, pl.ds(pl.multiple_of(me * TB, TB), TB)]
        dst = outs[a].at[:, pl.ds(pl.multiple_of(me * HD, HD), HD)]
        pltpu.make_async_copy(src, dst, loc.at[7 + a]).wait()


def on_device(
    self_query,
    self_key,
    self_value,
    cross_query,
    upstream,
    caption_ids,
    caption_lengths,
    embed_table,
    key_weight,
    value_weight,
):
    tokens = [x[0] for x in (self_query, self_key, self_value, cross_query, upstream)]
    anywhere = pl.BlockSpec(memory_space=pl.ANY)
    vmem = pl.BlockSpec(memory_space=pltpu.VMEM)
    smem = pl.BlockSpec(memory_space=pltpu.SMEM)
    token_grad = jax.ShapeDtypeStruct((TB, NS * HD), BF)
    weight_grad = jax.ShapeDtypeStruct((2, NY, 2, CW, HD), BF)
    n_gather = 25
    n_sum = 15
    dma = pltpu.SemaphoreType.DMA
    results = pl.pallas_call(
        kernel,
        out_shape=[token_grad] * 4 + [weight_grad] * 2,
        in_specs=[anywhere] * 5 + [vmem, smem, vmem, anywhere, anywhere],
        out_specs=[anywhere] * 6,
        scratch_shapes=[
            pltpu.VMEM((5, T, HD), BF),
            pltpu.VMEM((2, CW, VR), BF),
            pltpu.VMEM((NY, 2, CW, CAP), BF),
            pltpu.VMEM((2, 2, HC, CAP), BF),
            pltpu.VMEM((2, 2, CW, CAP), BF),
            pltpu.VMEM((CW, CAP), BF),
            pltpu.VMEM((NS, CW, CAP), BF),
            pltpu.VMEM((2 * HD, NS * CW), BF),
            pltpu.VMEM((2, NS * CW, HD), BF),
            pltpu.VMEM((T, BQ), F32),
            pltpu.VMEM((NQ, T, BQ), BF),
            pltpu.VMEM((NQ, 1, BQ), F32),
            pltpu.VMEM((HD, T), BF),
            pltpu.VMEM((2, T, HD), F32),
            pltpu.VMEM((4, T, HD), BF),
            pltpu.VMEM((2, CAP, HD), BF),
            pltpu.VMEM((HD, CAP), BF),
            pltpu.VMEM((CAP, 2 * HD), BF),
            pltpu.VMEM((NY, 2, CW, 2 * HD), BF),
            pltpu.VMEM((NY, 2, CW, 2 * HD), BF),
            pltpu.VMEM((NY, 2, CW, 2 * HD), F32),
            pltpu.VMEM((2, CW, 2 * HD), BF),
            pltpu.VMEM((2, 2, CW, 2 * HD), BF),
            pltpu.VMEM((2, 2, HC, 2 * HD), BF),
            pltpu.VMEM((2, 2, CW, 2 * HD), BF),
            pltpu.VMEM((CW, 2 * HD), BF),
            pltpu.VMEM((CW, 2 * HD), BF),
            pltpu.VMEM((2, NY, 2, CW, 2 * HD), BF),
            dma((5,)),
            dma((5,)),
            dma((13,)),
            dma((2,)),
            dma((5,)),
            dma((5,)),
            dma((n_gather,)),
            dma((n_gather,)),
            dma((4,)),
            dma((4,)),
            dma((n_sum,)),
            dma((n_sum,)),
        ],
        compiler_params=pltpu.CompilerParams(
            collective_id=0, has_side_effects=True, vmem_limit_bytes=56 * 1024 * 1024
        ),
    )(*tokens, caption_ids, caption_lengths, embed_table, key_weight, value_weight)
    rows = NS * CW
    return tuple(r[None] for r in results[:4]) + tuple(r.reshape(rows, HD) for r in results[4:])


def solution(mesh):
    placed = (
        P("dp", "seq", None),
        P("dp", "seq", None),
        P("dp", "seq", None),
        P("dp", "seq", None),
        P("dp", "seq", None),
        P(),
        P(),
        P("dp", "seq"),
        P(None, "seq"),
        P(None, "seq"),
    )
    return jax.shard_map(
        on_device,
        mesh=mesh,
        in_specs=placed,
        out_specs=(
            P("dp", "seq", None),
            P("dp", "seq", None),
            P("dp", "seq", None),
            P("dp", "seq", None),
            P(None, "seq"),
            P(None, "seq"),
        ),
        check_vma=False,
    )
```

```python
import math

import jax
import jax.numpy as jnp
from jax import lax
from jax.experimental import pallas as pl
from jax.experimental.pallas import tpu as pltpu
from jax.sharding import PartitionSpec as P

MESH = pl.DeviceIdType.MESH
BF = jnp.bfloat16
F32 = jnp.float32

NZ = 8
NS = 2 * NZ
NY = 4
HD = 128
TB = 128
T = NS * TB
CAP = 512
CW = 256
HC = CW // 2
VR = 1024
BQ = 256
NQ = T // BQ
KC = 256
SCALE = HD**-0.5
EARLY = (0, 1, 2)
AFTER = {"step1": (4,), "step3": (3,)}
LOG2 = SCALE * math.log2(math.e)


def nt(a, b):
    return lax.dot_general(a, b, (((1,), (1,)), ((), ())), preferred_element_type=F32)


def mm(a, b):
    return jnp.dot(a, b, preferred_element_type=F32)


def fold(x, op):
    return op(x.reshape(x.shape[0] // 8, 8, x.shape[1]), axis=0)


def kernel(
    sq, sk, sv, cq, up, ids, lens, table, kw, vw,
    oq, ok, ov, oc, gw,
    abuf, tabt, part, relay, rsy, emb, wt, wbuf, s_ref, e_ref, ec_ref, l_ref, kt, acc,
    dbuf, ckv, ckt, term, wsib, wcore, wown, wfar, wstep, wrelay, wry, wxs, wrx, agw,
    a_send, a_recv, loc, t_send, t_recv, y_send, y_recv, g_send, g_recv, o_send, o_recv, w_send, w_recv,
):
    me = lax.axis_index("seq")
    my_dp = lax.axis_index("dp")
    xl, z = me // NZ, me % NZ
    core = my_dp % 2
    chip = my_dp // 2
    xh, y = chip // NY, chip % NY

    def dp_of(x_at, y_at, c_at):
        return (x_at * NY + y_at) * 2 + c_at

    y_next, y_prev, y_far = (y + 1) % NY, (y + NY - 1) % NY, (y + 2) % NY
    sib = {"dp": dp_of(xh, y, 1 - core)}
    up_y = {"dp": dp_of(xh, y_next, core)}
    down_y = {"dp": dp_of(xh, y_prev, core)}
    over_x = {"dp": dp_of(1 - xh, y, core)}
    up_z = {"seq": xl * NZ + (z + 1) % NZ}
    down_z = {"seq": xl * NZ + (z + NZ - 1) % NZ}
    over_l = {"seq": (1 - xl) * NZ + z}

    def remote(src, dst, send, recv, device):
        return pltpu.make_async_remote_copy(
            src_ref=src, dst_ref=dst, send_sem=send, recv_sem=recv, device_id=device, device_id_type=MESH
        )

    barrier = pltpu.get_barrier_semaphore()

    def greet(k, carry):
        pl.semaphore_signal(barrier, inc=1, device_id={"seq": (me + k) % NS}, device_id_type=MESH)
        return carry

    lax.fori_loop(1, NS, greet, 0)
    for other in (sib, up_y, down_y, over_x):
        pl.semaphore_signal(barrier, inc=1, device_id=other, device_id_type=MESH)
    pl.semaphore_wait(barrier, NS - 1 + 4)

    tabt[0, core] = table[...].T
    table_over = remote(tabt.at[0, core], tabt.at[1, core], t_send.at[0], t_recv.at[0], over_x)
    table_over.start()
    table_sib = remote(tabt.at[0, core], tabt.at[0, core], t_send.at[1], t_recv.at[1], sib)
    table_sib.start()

    mine = pl.ds(pl.multiple_of(me * TB, TB), TB)
    sources = (sq, sk, up, sv, cq)

    def send_in(a, dx):
        src = sources[a]

        def send(step, carry):
            dz = (step + 1) // 2 * (2 * (step % 2) - 1)
            peer = (xl + dx) % 2 * NZ + (z + dz + NZ) % NZ
            remote(
                src.at[:, pl.ds(pl.multiple_of(peer * HD, HD), HD)],
                abuf.at[a, mine],
                a_send.at[a],
                a_recv.at[a],
                {"seq": peer},
            ).start()
            return carry

        lax.fori_loop(1 - dx, NZ, send, 0)

    for a in (0, 1, 2, 4, 3):
        pltpu.make_async_copy(
            sources[a].at[:, pl.ds(pl.multiple_of(me * HD, HD), HD)], abuf.at[a, mine], loc.at[a]
        ).start()
    for dx in range(2):
        for a in EARLY:
            send_in(a, dx)
    w_in = [pltpu.make_async_copy(w, wbuf.at[i], loc.at[5 + i]) for i, w in enumerate((kw, vw))]
    for copy in w_in:
        copy.start()

    def arrived(a):
        most = abuf.at[a, pl.ds(0, T - TB)]
        pltpu.make_async_copy(most, most, a_recv.at[a]).wait()
        pltpu.make_async_copy(
            sources[a].at[:, pl.ds(pl.multiple_of(me * HD, HD), HD)], abuf.at[a, mine], loc.at[a]
        ).wait()

    rows = lax.broadcasted_iota(jnp.int32, (KC, CAP), 0)

    def look(i, x_at, y_at):
        wanted = ids[pl.ds(dp_of(xh, y_at, core), 1), :] - dp_of(x_at, y, 0) * VR
        total = jnp.zeros((CW, CAP), F32)
        for half in range(2):
            for v in range(VR // KC):
                hot = jnp.where(rows == wanted - (half * VR + v * KC), 1.0, 0.0).astype(BF)
                total += mm(tabt[i, half, :, v * KC : (v + 1) * KC], hot)
        return total.astype(BF)

    def look_here(k, carry):
        y_at = (y + k) % NY
        part[y_at] = look(0, xh, y_at)
        return carry

    def look_there(k, carry):
        y_at = (y + k) % NY
        part[y_at] = part[y_at] + look(1, 1 - xh, y_at)
        return carry

    table_sib.wait_recv()
    lax.fori_loop(0, NY, look_here, 0)
    table_over.wait_recv()
    table_on = remote(tabt.at[1, core], tabt.at[1, core], t_send.at[2], t_recv.at[2], sib)
    table_on.start()

    for i, copy in enumerate(w_in):
        copy.wait()
        for j in range(NS):
            wt[i * HD : (i + 1) * HD, j * CW : (j + 1) * CW] = wbuf[i, j * CW : (j + 1) * CW, :].T

    low, high = pl.ds(0, HC), pl.ds(HC, HC)
    table_on.wait_recv()
    look_there(2, 0)
    far_up = remote(part.at[y_far, high], relay.at[0], y_send.at[0], y_recv.at[0], up_y)
    far_down = remote(part.at[y_far, low], relay.at[1], y_send.at[1], y_recv.at[1], down_y)
    far_up.start()
    far_down.start()
    look_there(1, 0)
    far_up.wait_recv()
    part[y_next, HC:] = part[y_next, HC:] + relay[0]
    near_up = remote(part.at[y_next], rsy.at[0], y_send.at[2], y_recv.at[2], up_y)
    near_up.start()
    look_there(3, 0)
    far_down.wait_recv()
    part[y_prev, :HC] = part[y_prev, :HC] + relay[1]
    near_down = remote(part.at[y_prev], rsy.at[1], y_send.at[3], y_recv.at[3], down_y)
    near_down.start()
    look_there(0, 0)
    near_up.wait_recv()
    near_down.wait_recv()

    def col(x_at, shift):
        return x_at * NZ + (z + shift + NZ) % NZ

    messages = {}

    def go(name, slot, part_rows, device):
        i = len(messages)
        ref = emb.at[slot] if part_rows is None else emb.at[slot, part_rows]
        messages[name] = remote(ref, ref, g_send.at[i], g_recv.at[i], device)
        messages[name].start()

    def got(name):
        messages[name].wait_recv()

    ox = 1 - xl

    def gather_start():
        emb[me] = part[y] + rsy[0] + rsy[1]
        go("pl1", me, low, up_z)
        go("ml1", me, low, down_z)
        go("xb", me, high, over_l)
        go("ph1", me, high, up_z)
        go("mh1", me, high, down_z)
        go("xa", me, low, over_l)

    def gather_step(k):
        if k > 0:
            got(f"pl{k}")
            got(f"ml{k}")
            go(f"pl{k + 1}", col(xl, -k), low, up_z)
            if k < 3:
                go(f"ml{k + 1}", col(xl, k), low, down_z)
            go(f"fp{k}", col(xl, -k), low, over_l)
            go(f"fm{k}", col(xl, k), low, over_l)
            got(f"ph{k}")
            got(f"mh{k}")
            if k < 3:
                go(f"ph{k + 1}", col(xl, -k), high, up_z)
            go(f"mh{k + 1}", col(xl, k), high, down_z)
            got(f"pb{k}")
            got(f"mb{k}")
        else:
            got("xb")
        if k < 3:
            go(f"pb{k + 1}", col(ox, -k), high, up_z)
            go(f"mb{k + 1}", col(ox, k), high, down_z)
        else:
            go("pb4", col(ox, -3), pl.ds(HC, HC // 2), up_z)
            go("mb4", col(ox, 3), pl.ds(HC + HC // 2, HC // 2), down_z)

    def gather_last():
        got("pl4")
        go("f4", col(xl, 4), low, over_l)

    def gather_end():
        for name in ("mh4", "xa", "pb4", "mb4", "fp1", "fm1", "fp2", "fm2", "fp3", "fm3", "f4"):
            got(name)

    def scores(queries, keys, n_keys, live):
        top = jnp.full((8, BQ), -jnp.inf, F32)
        for k in range(n_keys // KC):
            s = nt(keys[k * KC : (k + 1) * KC, :], queries)
            if live is not None:
                at = lax.broadcasted_iota(jnp.int32, (KC, BQ), 0) + k * KC
                s = jnp.where(at < live, s, -jnp.inf)
            s_ref[k * KC : (k + 1) * KC, :] = s
            top = jnp.maximum(top, fold(s, jnp.max))
        top = jnp.max(top, axis=0, keepdims=True) * LOG2
        total = jnp.zeros((8, BQ), F32)
        for k in range(n_keys // KC):
            e = jnp.exp2(s_ref[k * KC : (k + 1) * KC, :] * LOG2 - top)
            total += fold(e, jnp.sum)
            yield e.astype(BF)
        yield jnp.sum(total, axis=0, keepdims=True)

    def grads(queries, upstream, keys_t, values, n_keys, probs, total):
        inv = 1.0 / total
        delta = jnp.zeros((8, BQ), F32)
        for k in range(n_keys // KC):
            dp = nt(values[k * KC : (k + 1) * KC, :], upstream)
            s_ref[k * KC : (k + 1) * KC, :] = dp
            delta += fold(dp * probs[k * KC : (k + 1) * KC, :].astype(F32), jnp.sum)
        delta = jnp.sum(delta, axis=0, keepdims=True) * inv
        inv_rows = jnp.broadcast_to(inv, (HD, BQ)).T
        queries = (queries.astype(F32) * inv_rows).astype(BF)
        upstream = (upstream.astype(F32) * inv_rows).astype(BF)
        dq = jnp.zeros((HD, BQ), F32)
        for k in range(n_keys // KC):
            at = slice(k * KC, (k + 1) * KC)
            e = probs[at, :]
            ds = (e.astype(F32) * (s_ref[at, :] - delta)).astype(BF)
            dq += mm(keys_t[:, at], ds)
            acc[0, at, :] += mm(ds, queries)
            acc[1, at, :] += mm(e, upstream)
        return (dq * (inv * SCALE)).T.astype(BF)

    outs = (oq, ok, ov, oc)

    def post(a, peer):
        src = dbuf.at[a, pl.ds(pl.multiple_of(peer * TB, TB), TB)]
        dst = outs[a].at[:, pl.ds(pl.multiple_of(me * HD, HD), HD)]

        @pl.when(peer != me)
        def _():
            remote(src, dst, o_send.at[a], o_recv.at[a], {"seq": peer}).start()

        @pl.when(peer == me)
        def _():
            pltpu.make_async_copy(src, dst, loc.at[7 + a]).start()

    def first(q, carry):
        at = pl.ds(pl.multiple_of(q * BQ, BQ), BQ)
        for k, e in enumerate(scores(abuf[0, at, :], abuf.at[1], T, None)):
            if k < T // KC:
                e_ref[q, k * KC : (k + 1) * KC, :] = e
            else:
                l_ref[q] = e
        return carry

    def second(q, carry):
        at = pl.ds(pl.multiple_of(q * BQ, BQ), BQ)
        dbuf[0, at, :] = grads(
            abuf[0, at, :], abuf[2, at, :], kt, abuf.at[3], T, e_ref.at[q], l_ref[q]
        )
        for i in range(BQ // TB):
            post(0, q * (BQ // TB) + i)
        return carry

    def later(point):
        for a in AFTER.get(point, ()):
            for dx in range(2):
                send_in(a, dx)

    gather_start()
    later("start")
    arrived(0)
    arrived(1)
    for k in range(T // KC):
        kt[:, k * KC : (k + 1) * KC] = abuf[1, k * KC : (k + 1) * KC, :].T
    lax.fori_loop(0, 2, first, 0)
    gather_step(0)
    later("step0")
    lax.fori_loop(2, 4, first, 0)
    gather_step(1)
    later("step1")
    lax.fori_loop(4, 6, first, 0)
    gather_step(2)
    later("step2")
    lax.fori_loop(6, 8, first, 0)
    gather_step(3)
    later("step3")
    gather_last()

    gather_end()
    square = jnp.zeros((8, CAP), F32)
    kv = jnp.zeros((2 * HD, CAP), F32)
    for j in range(NS):
        block = emb[j]
        kv += mm(wt[:, j * CW : (j + 1) * CW], block)
        wide = block.astype(F32)
        square += fold(wide * wide, jnp.sum)
    mean = jnp.sum(square, axis=0, keepdims=True) * (1.0 / (NS * CW))
    rinv = lax.rsqrt(mean + 1e-06)
    kv = kv * rinv
    ckt[...] = kv[:HD, :].astype(BF)
    ckv[0] = kv[:HD, :].T.astype(BF)
    ckv[1] = kv[HD:, :].T.astype(BF)
    rinv_rows = jnp.broadcast_to(rinv, (HD, CAP)).T

    arrived(2)
    arrived(4)
    acc[:, :CAP, :] = jnp.zeros((2, CAP, HD), F32)
    live = lens[my_dp]

    def cross(q, carry):
        at = pl.ds(pl.multiple_of(q * BQ, BQ), BQ)
        queries = abuf[4, at, :]
        total = None
        for k, e in enumerate(scores(queries, ckv.at[0], CAP, live)):
            if k < CAP // KC:
                ec_ref[k * KC : (k + 1) * KC, :] = e
            else:
                total = e
        dbuf[3, at, :] = grads(
            queries, abuf[2, at, :], ckt, ckv.at[1], CAP, ec_ref, total
        )
        for i in range(BQ // TB):
            post(3, q * (BQ // TB) + i)
        return carry

    lax.fori_loop(0, NQ, cross, 0)

    term[:, :HD] = (acc[0, :CAP, :] * SCALE * rinv_rows).astype(BF)
    term[:, HD:] = (acc[1, :CAP, :] * rinv_rows).astype(BF)

    w_messages = []

    def hand(src, dst, device):
        i = len(w_messages)
        w_messages.append(remote(src, dst, w_send.at[i], w_recv.at[i], device))
        w_messages[i].start()
        return w_messages[i]

    def partial(base, out):
        def body(i, carry):
            out[i // 2, i % 2] = mm(emb[base + i], term[...]).astype(out.dtype)
            return carry

        lax.fori_loop(0, NZ, body, 0)

    def reduction(p):
        at = pl.ds(p * HD, HD)
        to_sib = hand(wsib.at[:, :, :, at], wcore.at[:, :, :, at], sib)
        if p == 0:
            partial(core * NZ, wown)
        yield
        to_sib.wait_recv()
        wfar[:, :, at] = (wown[y_far, :, :, at] + wcore[y_far, :, :, at].astype(F32)).astype(BF)
        f_up = hand(wfar.at[:, high, at], wrelay.at[0, :, :, at], up_y)
        f_down = hand(wfar.at[:, low, at], wrelay.at[1, :, :, at], down_y)
        for slot in (y_next, y_prev, y):
            wown[slot, :, :, at] = wown[slot, :, :, at] + wcore[slot, :, :, at].astype(F32)
        yield
        f_up.wait_recv()
        wstep[0, :, low, at] = wown[y_next, :, low, at].astype(BF)
        wstep[0, :, high, at] = (wown[y_next, :, high, at] + wrelay[0, :, :, at].astype(F32)).astype(BF)
        n_up = hand(wstep.at[0, :, :, at], wry.at[0, :, :, at], up_y)
        f_down.wait_recv()
        wstep[1, :, low, at] = (wown[y_prev, :, low, at] + wrelay[1, :, :, at].astype(F32)).astype(BF)
        wstep[1, :, high, at] = wown[y_prev, :, high, at].astype(BF)
        n_down = hand(wstep.at[1, :, :, at], wry.at[1, :, :, at], down_y)
        yield
        n_up.wait_recv()
        n_down.wait_recv()

        def here(x_at):
            return (
                wown[y, x_at, :, at]
                + wry[0, x_at, :, at].astype(F32)
                + wry[1, x_at, :, at].astype(F32)
            )

        wxs[:, at] = here(1 - xh).astype(BF)
        x_half = hand(wxs.at[:, at], wrx.at[:, at], over_x)
        mine_sum = here(xh)
        yield
        x_half.wait_recv()
        agw[core, y, xh, :, at] = (mine_sum + wrx[:, at].astype(F32)).astype(BF)
        own = agw.at[core, y, xh, :, at]
        x_back = hand(own, own, over_x)
        yield
        x_back.wait_recv()
        row = agw.at[core, y, :, :, at]
        b_up = hand(row, row, up_y)
        b_down = hand(row, row, down_y)
        backs = [hand(row, row, sib)]
        yield
        b_up.wait_recv()
        upper = agw.at[core, y_prev, :, high, at]
        c_up = hand(upper, upper, up_y)
        b_down.wait_recv()
        lower = agw.at[core, y_next, :, low, at]
        c_down = hand(lower, lower, down_y)
        for slot in (y_prev, y_next):
            block = agw.at[core, slot, :, :, at]
            backs.append(hand(block, block, sib))
        yield
        c_up.wait_recv()
        c_down.wait_recv()
        block = agw.at[core, y_far, :, :, at]
        backs.append(hand(block, block, sib))
        yield
        for message in backs:
            message.wait_recv()
        yield

    partial((1 - core) * NZ, wsib)
    sums = [reduction(0), reduction(1)]

    def stage():
        for part_sum in sums:
            next(part_sum)

    stage()
    arrived(3)
    acc[...] = jnp.zeros_like(acc)
    lax.fori_loop(0, 2, second, 0)
    stage()
    lax.fori_loop(2, 5, second, 0)
    stage()
    lax.fori_loop(5, 8, second, 0)
    dbuf[1] = (acc[0] * SCALE).astype(BF)
    dbuf[2] = acc[1].astype(BF)

    def post_kv(k, carry):
        peer = (me + k) % NS
        post(1, peer)
        post(2, peer)
        return carry

    lax.fori_loop(0, NS, post_kv, 0)
    for _ in range(6):
        stage()
    leave = [pltpu.make_async_copy(agw, gw, loc.at[11])]
    for copy in leave:
        copy.start()

    for copy in leave:
        copy.wait()
    tables = (table_over, table_sib, table_on)
    parts = (far_up, far_down, near_up, near_down)
    for message in (*tables, *parts, *messages.values(), *w_messages):
        message.wait_send()
    most = abuf.at[0, pl.ds(0, T - TB)]
    for a in range(5):
        pltpu.make_async_copy(most, most, a_send.at[a]).wait()
    for a in range(4):
        pltpu.make_async_copy(most, most, o_send.at[a]).wait()
        pltpu.make_async_copy(most, most, o_recv.at[a]).wait()
        src = dbuf.at[a, pl.ds(pl.multiple_of(me * TB, TB), TB)]
        dst = outs[a].at[:, pl.ds(pl.multiple_of(me * HD, HD), HD)]
        pltpu.make_async_copy(src, dst, loc.at[7 + a]).wait()


def leave_kernel(q, k, v, c, w, oq, ok, ov, oc, gk, gv):
    for src, dst in ((q, oq), (k, ok), (v, ov), (c, oc)):
        dst[0] = src[...]
    gk[...] = w[:, :HD]
    gv[...] = w[:, HD:]


def on_device(
    self_query,
    self_key,
    self_value,
    cross_query,
    upstream,
    caption_ids,
    caption_lengths,
    embed_table,
    key_weight,
    value_weight,
):
    tokens = [x[0] for x in (self_query, self_key, self_value, cross_query, upstream)]
    anywhere = pl.BlockSpec(memory_space=pl.ANY)
    vmem = pl.BlockSpec(memory_space=pltpu.VMEM)
    smem = pl.BlockSpec(memory_space=pltpu.SMEM)
    token_grad = jax.ShapeDtypeStruct((TB, NS * HD), BF)
    weight_grads = jax.ShapeDtypeStruct((2, NY, 2, CW, 2 * HD), BF)
    n_gather = 31
    n_sum = 30
    dma = pltpu.SemaphoreType.DMA
    results = pl.pallas_call(
        kernel,
        out_shape=[token_grad] * 4 + [weight_grads],
        in_specs=[anywhere] * 5 + [vmem, smem, vmem, anywhere, anywhere],
        out_specs=[anywhere] * 5,
        scratch_shapes=[
            pltpu.VMEM((5, T, HD), BF),
            pltpu.VMEM((2, 2, CW, VR), BF),
            pltpu.VMEM((NY, CW, CAP), BF),
            pltpu.VMEM((2, HC, CAP), BF),
            pltpu.VMEM((2, CW, CAP), BF),
            pltpu.VMEM((NS, CW, CAP), BF),
            pltpu.VMEM((2 * HD, NS * CW), BF),
            pltpu.VMEM((2, NS * CW, HD), BF),
            pltpu.VMEM((T, BQ), F32),
            pltpu.VMEM((NQ, T, BQ), BF),
            pltpu.VMEM((CAP, BQ), BF),
            pltpu.VMEM((NQ, 1, BQ), F32),
            pltpu.VMEM((HD, T), BF),
            pltpu.VMEM((2, T, HD), F32),
            pltpu.VMEM((4, T, HD), BF),
            pltpu.VMEM((2, CAP, HD), BF),
            pltpu.VMEM((HD, CAP), BF),
            pltpu.VMEM((CAP, 2 * HD), BF),
            pltpu.VMEM((NY, 2, CW, 2 * HD), BF),
            pltpu.VMEM((NY, 2, CW, 2 * HD), BF),
            pltpu.VMEM((NY, 2, CW, 2 * HD), F32),
            pltpu.VMEM((2, CW, 2 * HD), BF),
            pltpu.VMEM((2, 2, CW, 2 * HD), BF),
            pltpu.VMEM((2, 2, HC, 2 * HD), BF),
            pltpu.VMEM((2, 2, CW, 2 * HD), BF),
            pltpu.VMEM((CW, 2 * HD), BF),
            pltpu.VMEM((CW, 2 * HD), BF),
            pltpu.VMEM((2, NY, 2, CW, 2 * HD), BF),
            dma((5,)),
            dma((5,)),
            dma((12,)),
            dma((3,)),
            dma((3,)),
            dma((4,)),
            dma((4,)),
            dma((n_gather,)),
            dma((n_gather,)),
            dma((4,)),
            dma((4,)),
            dma((n_sum,)),
            dma((n_sum,)),
        ],
        compiler_params=pltpu.CompilerParams(
            collective_id=0, has_side_effects=True, vmem_limit_bytes=56 * 1024 * 1024
        ),
    )(*tokens, caption_ids, caption_lengths, embed_table, key_weight, value_weight)
    rows = NS * CW
    cuts = 4
    token_in = pl.BlockSpec((TB // cuts, NS * HD), lambda i: (i, 0))
    token_out = pl.BlockSpec((1, TB // cuts, NS * HD), lambda i: (0, i, 0))
    return pl.pallas_call(
        leave_kernel,
        grid=(cuts,),
        out_shape=[jax.ShapeDtypeStruct((1, TB, NS * HD), BF)] * 4
        + [jax.ShapeDtypeStruct((rows, HD), BF)] * 2,
        in_specs=[token_in] * 4 + [pl.BlockSpec((rows // cuts, 2 * HD), lambda i: (i, 0))],
        out_specs=[token_out] * 4 + [pl.BlockSpec((rows // cuts, HD), lambda i: (i, 0))] * 2,
    )(*results[:4], results[4].reshape(rows, 2 * HD))


def solution(mesh):
    placed = (
        P("dp", "seq", None),
        P("dp", "seq", None),
        P("dp", "seq", None),
        P("dp", "seq", None),
        P("dp", "seq", None),
        P(),
        P(),
        P("dp", "seq"),
        P(None, "seq"),
        P(None, "seq"),
    )
    return jax.shard_map(
        on_device,
        mesh=mesh,
        in_specs=placed,
        out_specs=(
            P("dp", "seq", None),
            P("dp", "seq", None),
            P("dp", "seq", None),
            P("dp", "seq", None),
            P(None, "seq"),
            P(None, "seq"),
        ),
        check_vma=False,
    )
```

```python
import math

import jax
import jax.numpy as jnp
from jax import lax
from jax.experimental import pallas as pl
from jax.experimental.pallas import tpu as pltpu
from jax.sharding import PartitionSpec as P

MESH = pl.DeviceIdType.MESH
BF = jnp.bfloat16
F32 = jnp.float32

NZ = 8
NS = 2 * NZ
NY = 4
HD = 128
TB = 128
T = NS * TB
CAP = 512
CW = 256
HC = CW // 2
VR = 1024
BQ = 256
NQ = T // BQ
KC = 256
SCALE = HD**-0.5
EARLY = (0, 1, 2)
AFTER = {"step1": (4,), "step3": (3,)}
LOG2 = SCALE * math.log2(math.e)


def nt(a, b):
    return lax.dot_general(a, b, (((1,), (1,)), ((), ())), preferred_element_type=F32)


def mm(a, b):
    return jnp.dot(a, b, preferred_element_type=F32)


def fold(x, op):
    return op(x.reshape(x.shape[0] // 8, 8, x.shape[1]), axis=0)


def kernel(
    sq, sk, sv, cq, up, ids, lens, table, kw, vw,
    oq, ok, ov, oc, gw,
    abuf, tabt, part, relay, rsy, emb, wt, wbuf, s_ref, e_ref, ec_ref, l_ref, kt, acc,
    dbuf, ckv, ckt, term, wsib, wcore, wown, wfar, wstep, wrelay, wry, wxs, wrx, agw,
    a_send, a_recv, loc, t_send, t_recv, y_send, y_recv, g_send, g_recv, o_send, o_recv, w_send, w_recv,
):
    me = lax.axis_index("seq")
    my_dp = lax.axis_index("dp")
    xl, z = me // NZ, me % NZ
    core = my_dp % 2
    chip = my_dp // 2
    xh, y = chip // NY, chip % NY

    def dp_of(x_at, y_at, c_at):
        return (x_at * NY + y_at) * 2 + c_at

    y_next, y_prev, y_far = (y + 1) % NY, (y + NY - 1) % NY, (y + 2) % NY
    sib = {"dp": dp_of(xh, y, 1 - core)}
    up_y = {"dp": dp_of(xh, y_next, core)}
    down_y = {"dp": dp_of(xh, y_prev, core)}
    over_x = {"dp": dp_of(1 - xh, y, core)}
    up_z = {"seq": xl * NZ + (z + 1) % NZ}
    down_z = {"seq": xl * NZ + (z + NZ - 1) % NZ}
    over_l = {"seq": (1 - xl) * NZ + z}

    def remote(src, dst, send, recv, device):
        return pltpu.make_async_remote_copy(
            src_ref=src, dst_ref=dst, send_sem=send, recv_sem=recv, device_id=device, device_id_type=MESH
        )

    barrier = pltpu.get_barrier_semaphore()

    def greet(k, carry):
        pl.semaphore_signal(barrier, inc=1, device_id={"seq": (me + k) % NS}, device_id_type=MESH)
        return carry

    lax.fori_loop(1, NS, greet, 0)
    for other in (sib, up_y, down_y, over_x):
        pl.semaphore_signal(barrier, inc=1, device_id=other, device_id_type=MESH)
    pl.semaphore_wait(barrier, NS - 1 + 4)

    mine = pl.ds(pl.multiple_of(me * TB, TB), TB)
    sources = (sq, sk, up, sv, cq)

    def send_in(a, dx):
        src = sources[a]

        def send(step, carry):
            dz = (step + 1) // 2 * (2 * (step % 2) - 1)
            peer = (xl + dx) % 2 * NZ + (z + dz + NZ) % NZ
            remote(
                src.at[:, pl.ds(pl.multiple_of(peer * HD, HD), HD)],
                abuf.at[a, mine],
                a_send.at[a],
                a_recv.at[a],
                {"seq": peer},
            ).start()
            return carry

        lax.fori_loop(1 - dx, NZ, send, 0)

    for a in (0, 1, 2, 4, 3):
        pltpu.make_async_copy(
            sources[a].at[:, pl.ds(pl.multiple_of(me * HD, HD), HD)], abuf.at[a, mine], loc.at[a]
        ).start()
    send_in(0, 0)

    tabt[0, core] = table[...].T
    table_over = remote(tabt.at[0, core], tabt.at[1, core], t_send.at[0], t_recv.at[0], over_x)
    table_over.start()
    table_sib = remote(tabt.at[0, core], tabt.at[0, core], t_send.at[1], t_recv.at[1], sib)
    table_sib.start()

    for dx in range(2):
        for a in EARLY:
            if (a, dx) != (0, 0):
                send_in(a, dx)
    w_in = [pltpu.make_async_copy(w, wbuf.at[i], loc.at[5 + i]) for i, w in enumerate((kw, vw))]
    for copy in w_in:
        copy.start()

    def arrived(a):
        most = abuf.at[a, pl.ds(0, T - TB)]
        pltpu.make_async_copy(most, most, a_recv.at[a]).wait()
        pltpu.make_async_copy(
            sources[a].at[:, pl.ds(pl.multiple_of(me * HD, HD), HD)], abuf.at[a, mine], loc.at[a]
        ).wait()

    rows = lax.broadcasted_iota(jnp.int32, (KC, CAP), 0)

    def look(i, x_at, y_at):
        wanted = ids[pl.ds(dp_of(xh, y_at, core), 1), :] - dp_of(x_at, y, 0) * VR
        total = jnp.zeros((CW, CAP), F32)
        for half in range(2):
            for v in range(VR // KC):
                hot = jnp.where(rows == wanted - (half * VR + v * KC), 1.0, 0.0).astype(BF)
                total += mm(tabt[i, half, :, v * KC : (v + 1) * KC], hot)
        return total.astype(BF)

    def look_here(k, carry):
        y_at = (y + k) % NY
        part[y_at] = look(0, xh, y_at)
        return carry

    def look_there(k, carry):
        y_at = (y + k) % NY
        part[y_at] = part[y_at] + look(1, 1 - xh, y_at)
        return carry

    table_sib.wait_recv()
    lax.fori_loop(0, NY, look_here, 0)
    table_over.wait_recv()
    table_on = remote(tabt.at[1, core], tabt.at[1, core], t_send.at[2], t_recv.at[2], sib)
    table_on.start()

    low, high = pl.ds(0, HC), pl.ds(HC, HC)
    table_on.wait_recv()
    look_there(2, 0)
    far_up = remote(part.at[y_far, high], relay.at[0], y_send.at[0], y_recv.at[0], up_y)
    far_down = remote(part.at[y_far, low], relay.at[1], y_send.at[1], y_recv.at[1], down_y)
    far_up.start()
    far_down.start()
    look_there(1, 0)
    far_up.wait_recv()
    part[y_next, HC:] = part[y_next, HC:] + relay[0]
    near_up = remote(part.at[y_next], rsy.at[0], y_send.at[2], y_recv.at[2], up_y)
    near_up.start()
    look_there(3, 0)
    far_down.wait_recv()
    part[y_prev, :HC] = part[y_prev, :HC] + relay[1]
    near_down = remote(part.at[y_prev], rsy.at[1], y_send.at[3], y_recv.at[3], down_y)
    near_down.start()
    look_there(0, 0)
    near_up.wait_recv()
    near_down.wait_recv()

    def col(x_at, shift):
        return x_at * NZ + (z + shift + NZ) % NZ

    messages = {}

    def go(name, slot, part_rows, device):
        i = len(messages)
        ref = emb.at[slot] if part_rows is None else emb.at[slot, part_rows]
        messages[name] = remote(ref, ref, g_send.at[i], g_recv.at[i], device)
        messages[name].start()

    def got(name):
        messages[name].wait_recv()

    ox = 1 - xl

    def gather_start():
        emb[me] = part[y] + rsy[0] + rsy[1]
        go("pl1", me, low, up_z)
        go("ml1", me, low, down_z)
        go("xb", me, high, over_l)
        go("ph1", me, high, up_z)
        go("mh1", me, high, down_z)
        go("xa", me, low, over_l)

    def gather_step(k):
        if k > 0:
            got(f"pl{k}")
            got(f"ml{k}")
            go(f"pl{k + 1}", col(xl, -k), low, up_z)
            if k < 3:
                go(f"ml{k + 1}", col(xl, k), low, down_z)
            go(f"fp{k}", col(xl, -k), low, over_l)
            go(f"fm{k}", col(xl, k), low, over_l)
            got(f"ph{k}")
            got(f"mh{k}")
            if k < 3:
                go(f"ph{k + 1}", col(xl, -k), high, up_z)
            go(f"mh{k + 1}", col(xl, k), high, down_z)
            got(f"pb{k}")
            got(f"mb{k}")
        else:
            got("xb")
        if k < 3:
            go(f"pb{k + 1}", col(ox, -k), high, up_z)
            go(f"mb{k + 1}", col(ox, k), high, down_z)
        else:
            go("pb4", col(ox, -3), pl.ds(HC, HC // 2), up_z)
            go("mb4", col(ox, 3), pl.ds(HC + HC // 2, HC // 2), down_z)

    def gather_last():
        got("pl4")
        go("f4", col(xl, 4), low, over_l)

    def gather_end():
        for name in ("mh4", "xa", "pb4", "mb4", "fp1", "fm1", "fp2", "fm2", "fp3", "fm3", "f4"):
            got(name)

    def scores(queries, keys, n_keys, live):
        top = jnp.full((8, BQ), -jnp.inf, F32)
        for k in range(n_keys // KC):
            s = nt(keys[k * KC : (k + 1) * KC, :], queries)
            if live is not None:
                at = lax.broadcasted_iota(jnp.int32, (KC, BQ), 0) + k * KC
                s = jnp.where(at < live, s, -jnp.inf)
            s_ref[k * KC : (k + 1) * KC, :] = s
            top = jnp.maximum(top, fold(s, jnp.max))
        top = jnp.max(top, axis=0, keepdims=True) * LOG2
        total = jnp.zeros((8, BQ), F32)
        for k in range(n_keys // KC):
            e = jnp.exp2(s_ref[k * KC : (k + 1) * KC, :] * LOG2 - top)
            total += fold(e, jnp.sum)
            yield e.astype(BF)
        yield jnp.sum(total, axis=0, keepdims=True)

    def grads(queries, upstream, keys_t, values, n_keys, probs, total):
        inv = 1.0 / total
        delta = jnp.zeros((8, BQ), F32)
        for k in range(n_keys // KC):
            dp = nt(values[k * KC : (k + 1) * KC, :], upstream)
            s_ref[k * KC : (k + 1) * KC, :] = dp
            delta += fold(dp * probs[k * KC : (k + 1) * KC, :].astype(F32), jnp.sum)
        delta = jnp.sum(delta, axis=0, keepdims=True) * inv
        inv_rows = jnp.broadcast_to(inv, (HD, BQ)).T
        queries = (queries.astype(F32) * inv_rows).astype(BF)
        upstream = (upstream.astype(F32) * inv_rows).astype(BF)
        dq = jnp.zeros((HD, BQ), F32)
        for k in range(n_keys // KC):
            at = slice(k * KC, (k + 1) * KC)
            e = probs[at, :]
            ds = (e.astype(F32) * (s_ref[at, :] - delta)).astype(BF)
            dq += mm(keys_t[:, at], ds)
            acc[0, at, :] += mm(ds, queries)
            acc[1, at, :] += mm(e, upstream)
        return (dq * (inv * SCALE)).T.astype(BF)

    outs = (oq, ok, ov, oc)

    def post(a, peer):
        src = dbuf.at[a, pl.ds(pl.multiple_of(peer * TB, TB), TB)]
        dst = outs[a].at[:, pl.ds(pl.multiple_of(me * HD, HD), HD)]

        @pl.when(peer != me)
        def _():
            remote(src, dst, o_send.at[a], o_recv.at[a], {"seq": peer}).start()

        @pl.when(peer == me)
        def _():
            pltpu.make_async_copy(src, dst, loc.at[7 + a]).start()

    def first(q, carry):
        at = pl.ds(pl.multiple_of(q * BQ, BQ), BQ)
        for k, e in enumerate(scores(abuf[0, at, :], abuf.at[1], T, None)):
            if k < T // KC:
                e_ref[q, k * KC : (k + 1) * KC, :] = e
            else:
                l_ref[q] = e
        return carry

    def second(q, carry):
        at = pl.ds(pl.multiple_of(q * BQ, BQ), BQ)
        dbuf[0, at, :] = grads(
            abuf[0, at, :], abuf[2, at, :], kt, abuf.at[3], T, e_ref.at[q], l_ref[q]
        )
        for i in range(BQ // TB):
            post(0, q * (BQ // TB) + i)
        return carry

    def later(point):
        for a in AFTER.get(point, ()):
            for dx in range(2):
                send_in(a, dx)

    gather_start()
    later("start")
    for i, copy in enumerate(w_in):
        copy.wait()
        for j in range(NS):
            wt[i * HD : (i + 1) * HD, j * CW : (j + 1) * CW] = wbuf[i, j * CW : (j + 1) * CW, :].T
    gather_step(0)
    later("step0")
    arrived(0)
    arrived(1)
    for k in range(T // KC):
        kt[:, k * KC : (k + 1) * KC] = abuf[1, k * KC : (k + 1) * KC, :].T
    lax.fori_loop(0, 3, first, 0)
    gather_step(1)
    later("step1")
    lax.fori_loop(3, 6, first, 0)
    gather_step(2)
    later("step2")
    lax.fori_loop(6, 8, first, 0)
    gather_step(3)
    later("step3")
    gather_last()

    gather_end()
    square = jnp.zeros((8, CAP), F32)
    kv = jnp.zeros((2 * HD, CAP), F32)
    for j in range(NS):
        block = emb[j]
        kv += mm(wt[:, j * CW : (j + 1) * CW], block)
        wide = block.astype(F32)
        square += fold(wide * wide, jnp.sum)
    mean = jnp.sum(square, axis=0, keepdims=True) * (1.0 / (NS * CW))
    rinv = lax.rsqrt(mean + 1e-06)
    kv = kv * rinv
    ckt[...] = kv[:HD, :].astype(BF)
    ckv[0] = kv[:HD, :].T.astype(BF)
    ckv[1] = kv[HD:, :].T.astype(BF)
    rinv_rows = jnp.broadcast_to(rinv, (HD, CAP)).T

    arrived(2)
    arrived(4)
    acc[:, :CAP, :] = jnp.zeros((2, CAP, HD), F32)
    live = lens[my_dp]

    def cross(q, carry):
        at = pl.ds(pl.multiple_of(q * BQ, BQ), BQ)
        queries = abuf[4, at, :]
        total = None
        for k, e in enumerate(scores(queries, ckv.at[0], CAP, live)):
            if k < CAP // KC:
                ec_ref[k * KC : (k + 1) * KC, :] = e
            else:
                total = e
        dbuf[3, at, :] = grads(
            queries, abuf[2, at, :], ckt, ckv.at[1], CAP, ec_ref, total
        )
        for i in range(BQ // TB):
            post(3, q * (BQ // TB) + i)
        return carry

    lax.fori_loop(0, NQ, cross, 0)

    term[:, :HD] = (acc[0, :CAP, :] * SCALE * rinv_rows).astype(BF)
    term[:, HD:] = (acc[1, :CAP, :] * rinv_rows).astype(BF)

    w_messages = []

    def hand(src, dst, device):
        i = len(w_messages)
        w_messages.append(remote(src, dst, w_send.at[i], w_recv.at[i], device))
        w_messages[i].start()
        return w_messages[i]

    def partial(base, out):
        def body(i, carry):
            out[i // 2, i % 2] = mm(emb[base + i], term[...]).astype(out.dtype)
            return carry

        lax.fori_loop(0, NZ, body, 0)

    def reduction(p):
        at = pl.ds(p * HD, HD)
        to_sib = hand(wsib.at[:, :, :, at], wcore.at[:, :, :, at], sib)
        if p == 0:
            partial(core * NZ, wown)
        yield
        to_sib.wait_recv()
        wfar[:, :, at] = (wown[y_far, :, :, at] + wcore[y_far, :, :, at].astype(F32)).astype(BF)
        f_up = hand(wfar.at[:, high, at], wrelay.at[0, :, :, at], up_y)
        f_down = hand(wfar.at[:, low, at], wrelay.at[1, :, :, at], down_y)
        for slot in (y_next, y_prev, y):
            wown[slot, :, :, at] = wown[slot, :, :, at] + wcore[slot, :, :, at].astype(F32)
        yield
        f_up.wait_recv()
        wstep[0, :, low, at] = wown[y_next, :, low, at].astype(BF)
        wstep[0, :, high, at] = (wown[y_next, :, high, at] + wrelay[0, :, :, at].astype(F32)).astype(BF)
        n_up = hand(wstep.at[0, :, :, at], wry.at[0, :, :, at], up_y)
        f_down.wait_recv()
        wstep[1, :, low, at] = (wown[y_prev, :, low, at] + wrelay[1, :, :, at].astype(F32)).astype(BF)
        wstep[1, :, high, at] = wown[y_prev, :, high, at].astype(BF)
        n_down = hand(wstep.at[1, :, :, at], wry.at[1, :, :, at], down_y)
        yield
        n_up.wait_recv()
        n_down.wait_recv()

        def here(x_at):
            return (
                wown[y, x_at, :, at]
                + wry[0, x_at, :, at].astype(F32)
                + wry[1, x_at, :, at].astype(F32)
            )

        wxs[:, at] = here(1 - xh).astype(BF)
        x_half = hand(wxs.at[:, at], wrx.at[:, at], over_x)
        mine_sum = here(xh)
        yield
        x_half.wait_recv()
        agw[core, y, xh, :, at] = (mine_sum + wrx[:, at].astype(F32)).astype(BF)
        own = agw.at[core, y, xh, :, at]
        x_back = hand(own, own, over_x)
        yield
        x_back.wait_recv()
        row = agw.at[core, y, :, :, at]
        b_up = hand(row, row, up_y)
        b_down = hand(row, row, down_y)
        backs = [hand(row, row, sib)]
        yield
        b_up.wait_recv()
        upper = agw.at[core, y_prev, :, high, at]
        c_up = hand(upper, upper, up_y)
        b_down.wait_recv()
        lower = agw.at[core, y_next, :, low, at]
        c_down = hand(lower, lower, down_y)
        for slot in (y_prev, y_next):
            block = agw.at[core, slot, :, :, at]
            backs.append(hand(block, block, sib))
        yield
        c_up.wait_recv()
        c_down.wait_recv()
        block = agw.at[core, y_far, :, :, at]
        backs.append(hand(block, block, sib))
        yield
        for message in backs:
            message.wait_recv()
        yield

    partial((1 - core) * NZ, wsib)
    sums = [reduction(0), reduction(1)]

    def stage():
        for part_sum in sums:
            next(part_sum)

    stage()
    arrived(3)
    acc[...] = jnp.zeros_like(acc)
    lax.fori_loop(0, 2, second, 0)
    stage()
    lax.fori_loop(2, 5, second, 0)
    stage()
    lax.fori_loop(5, 8, second, 0)
    dbuf[1] = (acc[0] * SCALE).astype(BF)
    dbuf[2] = acc[1].astype(BF)

    def post_kv(k, carry):
        peer = (me + k) % NS
        post(1, peer)
        post(2, peer)
        return carry

    lax.fori_loop(0, NS, post_kv, 0)
    for _ in range(6):
        stage()
    leave = [pltpu.make_async_copy(agw, gw, loc.at[11])]
    for copy in leave:
        copy.start()

    for copy in leave:
        copy.wait()
    tables = (table_over, table_sib, table_on)
    parts = (far_up, far_down, near_up, near_down)
    for message in (*tables, *parts, *messages.values(), *w_messages):
        message.wait_send()
    most = abuf.at[0, pl.ds(0, T - TB)]
    for a in range(5):
        pltpu.make_async_copy(most, most, a_send.at[a]).wait()
    for a in range(4):
        pltpu.make_async_copy(most, most, o_send.at[a]).wait()
        pltpu.make_async_copy(most, most, o_recv.at[a]).wait()
        src = dbuf.at[a, pl.ds(pl.multiple_of(me * TB, TB), TB)]
        dst = outs[a].at[:, pl.ds(pl.multiple_of(me * HD, HD), HD)]
        pltpu.make_async_copy(src, dst, loc.at[7 + a]).wait()


def leave_kernel(q, k, v, c, w, oq, ok, ov, oc, gk, gv):
    for src, dst in ((q, oq), (k, ok), (v, ov), (c, oc)):
        dst[0] = src[...]
    gk[...] = w[:, :HD]
    gv[...] = w[:, HD:]


def on_device(
    self_query,
    self_key,
    self_value,
    cross_query,
    upstream,
    caption_ids,
    caption_lengths,
    embed_table,
    key_weight,
    value_weight,
):
    tokens = [x[0] for x in (self_query, self_key, self_value, cross_query, upstream)]
    anywhere = pl.BlockSpec(memory_space=pl.ANY)
    vmem = pl.BlockSpec(memory_space=pltpu.VMEM)
    smem = pl.BlockSpec(memory_space=pltpu.SMEM)
    token_grad = jax.ShapeDtypeStruct((TB, NS * HD), BF)
    weight_grads = jax.ShapeDtypeStruct((2, NY, 2, CW, 2 * HD), BF)
    n_gather = 31
    n_sum = 30
    dma = pltpu.SemaphoreType.DMA
    results = pl.pallas_call(
        kernel,
        out_shape=[token_grad] * 4 + [weight_grads],
        in_specs=[anywhere] * 5 + [vmem, smem, vmem, anywhere, anywhere],
        out_specs=[anywhere] * 5,
        scratch_shapes=[
            pltpu.VMEM((5, T, HD), BF),
            pltpu.VMEM((2, 2, CW, VR), BF),
            pltpu.VMEM((NY, CW, CAP), BF),
            pltpu.VMEM((2, HC, CAP), BF),
            pltpu.VMEM((2, CW, CAP), BF),
            pltpu.VMEM((NS, CW, CAP), BF),
            pltpu.VMEM((2 * HD, NS * CW), BF),
            pltpu.VMEM((2, NS * CW, HD), BF),
            pltpu.VMEM((T, BQ), F32),
            pltpu.VMEM((NQ, T, BQ), BF),
            pltpu.VMEM((CAP, BQ), BF),
            pltpu.VMEM((NQ, 1, BQ), F32),
            pltpu.VMEM((HD, T), BF),
            pltpu.VMEM((2, T, HD), F32),
            pltpu.VMEM((4, T, HD), BF),
            pltpu.VMEM((2, CAP, HD), BF),
            pltpu.VMEM((HD, CAP), BF),
            pltpu.VMEM((CAP, 2 * HD), BF),
            pltpu.VMEM((NY, 2, CW, 2 * HD), BF),
            pltpu.VMEM((NY, 2, CW, 2 * HD), BF),
            pltpu.VMEM((NY, 2, CW, 2 * HD), F32),
            pltpu.VMEM((2, CW, 2 * HD), BF),
            pltpu.VMEM((2, 2, CW, 2 * HD), BF),
            pltpu.VMEM((2, 2, HC, 2 * HD), BF),
            pltpu.VMEM((2, 2, CW, 2 * HD), BF),
            pltpu.VMEM((CW, 2 * HD), BF),
            pltpu.VMEM((CW, 2 * HD), BF),
            pltpu.VMEM((2, NY, 2, CW, 2 * HD), BF),
            dma((5,)),
            dma((5,)),
            dma((12,)),
            dma((3,)),
            dma((3,)),
            dma((4,)),
            dma((4,)),
            dma((n_gather,)),
            dma((n_gather,)),
            dma((4,)),
            dma((4,)),
            dma((n_sum,)),
            dma((n_sum,)),
        ],
        compiler_params=pltpu.CompilerParams(
            collective_id=0, has_side_effects=True, vmem_limit_bytes=56 * 1024 * 1024
        ),
    )(*tokens, caption_ids, caption_lengths, embed_table, key_weight, value_weight)
    rows = NS * CW
    cuts = 4
    token_in = pl.BlockSpec((TB // cuts, NS * HD), lambda i: (i, 0))
    token_out = pl.BlockSpec((1, TB // cuts, NS * HD), lambda i: (0, i, 0))
    return pl.pallas_call(
        leave_kernel,
        grid=(cuts,),
        out_shape=[jax.ShapeDtypeStruct((1, TB, NS * HD), BF)] * 4
        + [jax.ShapeDtypeStruct((rows, HD), BF)] * 2,
        in_specs=[token_in] * 4 + [pl.BlockSpec((rows // cuts, 2 * HD), lambda i: (i, 0))],
        out_specs=[token_out] * 4 + [pl.BlockSpec((rows // cuts, HD), lambda i: (i, 0))] * 2,
    )(*results[:4], results[4].reshape(rows, 2 * HD))


def solution(mesh):
    placed = (
        P("dp", "seq", None),
        P("dp", "seq", None),
        P("dp", "seq", None),
        P("dp", "seq", None),
        P("dp", "seq", None),
        P(),
        P(),
        P("dp", "seq"),
        P(None, "seq"),
        P(None, "seq"),
    )
    return jax.shard_map(
        on_device,
        mesh=mesh,
        in_specs=placed,
        out_specs=(
            P("dp", "seq", None),
            P("dp", "seq", None),
            P("dp", "seq", None),
            P("dp", "seq", None),
            P(None, "seq"),
            P(None, "seq"),
        ),
        check_vma=False,
    )
```
